128 devices in a mesh: leaf: 16 (over x, y), rep: 8 (over z, core).
Axes of the slice: x: 4, y: 4, z: 4, core: 2. Of those that a mesh axis runs over, the one named last changes fastest.
Arguments:
- queries: bfloat16 [128, 256, 4096], P(('leaf', 'rep')), may hold values from -128 to 128
- attn_out: bfloat16 [128, 256, 4096], P(('leaf', 'rep')), may hold values from -6 to 6
- grad_out: bfloat16 [128, 256, 4096], P(('leaf', 'rep')), may hold values from -6 to 6
- seg_keys: bfloat16 [128, 256, 512], P(('leaf', 'rep')), may hold values from -6 to 6
- seg_values: bfloat16 [128, 256, 512], P(('leaf', 'rep')), may hold values from -6 to 6
- root_keys: bfloat16 [2048, 512], P('leaf'), may hold values from -6 to 6
- root_values: bfloat16 [2048, 512], P('leaf'), may hold values from -6 to 6
- parent: int32 [128], replicated, may hold values from -1 to 13, as said below
- seg_blocks: int32 [128], replicated, may hold values from 1 to 2
Outputs:
- grad_queries: bfloat16 [128, 256, 4096], P(('leaf', 'rep'))
- grad_seg_keys: bfloat16 [128, 256, 512], P(('leaf', 'rep'))
- grad_seg_values: bfloat16 [128, 256, 512], P(('leaf', 'rep'))
- grad_root_keys: bfloat16 [2048, 512], P('leaf')
- grad_root_values: bfloat16 [2048, 512], P('leaf')
The draws below stay inside these ranges and needn't reach their ends.
Inputs may be any that keep to these rules, and one draw needn't show every extreme that they name: Leaf index l of a row holds depth l % 3: depth 0 segments hang below the root, a segment of depth 1 or 2 has as parent a smaller leaf index of depth one less.
All inputs are finite; a program needn't handle non-finite values.
Results may differ from the reference program's by a relative error of at most 0.014.
Values may be sent and summed in bfloat16 or wider, within the bound.
No kernel may reach another device: no remote copies, remote signals or barrier semaphores. Data moves between devices by JAX's collectives and lax.ppermute only.
A program may use at most 192 MiB of HBM per device.

```python
import math
import jax
import jax.numpy as jnp
from jax import lax

HEADS = 32
KV_HEADS = 4
HEAD_DIM = 128
BLOCK = 128
SEG_BLK = 2
SEG_TOK = 256
ROOT = 2048
SEGS = 128
N_REP = 8


def root_rows(key):
    noise = jax.random.normal(jax.random.fold_in(key, 101), (ROOT, KV_HEADS * HEAD_DIM), jnp.float32)
    return jnp.clip(noise, -6.0, 6.0)


def draw_root_keys(key, part):
    base = root_rows(key)
    return base.astype(jnp.bfloat16)


def draw_queries(key, part):
    key = jax.random.fold_in(key, 2)
    key_a = jax.random.fold_in(key, 0)
    drawn = jnp.clip(jax.random.normal(key_a, (SEGS, SEG_TOK, HEADS * HEAD_DIM), jnp.float32), -6.0, 6.0)
    return drawn.astype(jnp.bfloat16)


def draw_parent(key, part):
    key = jax.random.fold_in(key, 3)
    seg_ids = jnp.arange(SEGS, dtype=jnp.int32)
    leaves = seg_ids // N_REP
    depth = leaves % 3
    choices_count = jnp.maximum((leaves - depth) // 3 + 1, 1)
    picked = jax.random.randint(key, (SEGS,), 0, choices_count)
    picked = jnp.where(seg_ids % N_REP == 0, choices_count - 1, picked)
    return jnp.where(depth == 0, -1, 3 * picked + depth - 1).astype(jnp.int32)


def draw_seg_blocks(key, part):
    key = jax.random.fold_in(key, 4)
    lengths = jax.random.randint(key, (SEGS,), 1, SEG_BLK + 1)
    return lengths.at[0].set(SEG_BLK).astype(jnp.int32)


def shard_levels(stream_key, extent, pieces, low, largest):
    loudness = 1.0
    for position, shards_of in pieces:
        steps = jax.random.uniform(jax.random.fold_in(jax.random.fold_in(stream_key, 6), position), (shards_of,), jnp.float32, low / len(pieces), largest / len(pieces))
        loudness = loudness * jnp.repeat(jnp.exp(steps), extent[position] // shards_of).reshape((-1,) + (1,) * (len(extent) - 1 - position))
    return loudness


def gaussian(key, extent, scale, bound, pieces=(), held_as=jnp.bfloat16):
    entries = jax.random.normal(key, extent, jnp.float32) * scale
    if len(pieces) > 0:
        entries = shard_levels(key, extent, pieces, -0.22, 0.18) * entries
    return jnp.clip(entries, min=-bound, max=bound).astype(held_as)


def setup_inputs(seed: int = 0) -> dict:
    key_of = jax.random.split(jax.random.key(seed), 10)
    return {
        "queries": draw_queries(jax.random.fold_in(key_of[9], 71), 0),
        "attn_out": gaussian(key_of[1], (SEGS, SEG_TOK, HEADS * HEAD_DIM), 1.0, 6.0, ((0, 128),)),
        "grad_out": gaussian(key_of[2], (SEGS, SEG_TOK, HEADS * HEAD_DIM), 1.0, 6.0, ((0, 128),)),
        "seg_keys": gaussian(key_of[3], (SEGS, SEG_TOK, KV_HEADS * HEAD_DIM), 1.0, 6.0, ((0, 128),)),
        "seg_values": gaussian(key_of[4], (SEGS, SEG_TOK, KV_HEADS * HEAD_DIM), 1.0, 6.0, ((0, 128),)),
        "root_keys": draw_root_keys(jax.random.fold_in(key_of[9], 71), 0),
        "root_values": gaussian(key_of[6], (ROOT, KV_HEADS * HEAD_DIM), 1.0, 6.0, ((0, 16),)),
        "parent": draw_parent(jax.random.fold_in(key_of[9], 71), 0),
        "seg_blocks": draw_seg_blocks(jax.random.fold_in(key_of[9], 71), 0),
    }


def round_half(values):
    return lax.optimization_barrier(values.astype(jnp.bfloat16)).astype(jnp.float32)

def attend_back(query_rows, out_rows, grad_rows, key_rows, value_rows, key_mask):
    tokens = query_rows.shape[0]
    count = key_rows.shape[0]
    group_size = HEADS // KV_HEADS
    scale = 1.0 / math.sqrt(HEAD_DIM)
    query4 = query_rows.astype(jnp.float32).reshape(tokens, KV_HEADS, group_size, HEAD_DIM)
    out4 = out_rows.astype(jnp.float32).reshape(tokens, KV_HEADS, group_size, HEAD_DIM)
    grad4 = grad_rows.astype(jnp.float32).reshape(tokens, KV_HEADS, group_size, HEAD_DIM)
    keys3 = key_rows.astype(jnp.float32).reshape(count, KV_HEADS, HEAD_DIM)
    values3 = value_rows.astype(jnp.float32).reshape(count, KV_HEADS, HEAD_DIM)
    scores = jnp.einsum('tcgd,ncd->cgtn', query4, keys3) * scale
    scores = jnp.where(key_mask[None, None], scores, -jnp.inf)
    row_max = lax.optimization_barrier(jnp.max(scores, axis=-1, keepdims=True))
    expo = jnp.exp(scores - row_max)
    weights = expo / lax.optimization_barrier(jnp.sum(expo, axis=-1, keepdims=True))
    delta_row = jnp.transpose(lax.optimization_barrier(jnp.sum(grad4 * out4, axis=-1)), (1, 2, 0))[..., None]
    dprobs = jnp.einsum('tcgd,ncd->cgtn', grad4, values3)
    dscores = round_half(weights * (dprobs - delta_row) * scale)
    weight_half = round_half(weights)
    grad_q = jnp.einsum('cgtn,ncd->tcgd', dscores, keys3).reshape(tokens, -1)
    grad_k = jnp.einsum('cgtn,tcgd->ncd', dscores, query4).reshape(count, -1)
    grad_v = jnp.einsum('cgtn,tcgd->ncd', weight_half, grad4).reshape(count, -1)
    return (grad_q, grad_k, grad_v)

def reference(queries, attn_out, grad_out, seg_keys, seg_values, root_keys, root_values, parent, seg_blocks):
    positions = jnp.arange(SEG_TOK, dtype=jnp.int32)
    width = KV_HEADS * HEAD_DIM

    def segment_step(totals, seg_id):
        root_gk, root_gv, seg_gk, seg_gv = totals
        rep_pos = seg_id % N_REP
        parent_one = parent[seg_id]
        one_at = jnp.maximum(parent_one, 0) * N_REP + rep_pos
        parent_two = jnp.where(parent_one >= 0, parent[one_at], -1).astype(jnp.int32)
        two_at = jnp.maximum(parent_two, 0) * N_REP + rep_pos
        one_len = jnp.where(parent_one >= 0, seg_blocks[one_at] * BLOCK, 0)
        two_len = jnp.where(parent_two >= 0, seg_blocks[two_at] * BLOCK, 0)
        own_len = seg_blocks[seg_id] * BLOCK
        key_rows = jnp.concatenate([root_keys, seg_keys[two_at], seg_keys[one_at], seg_keys[seg_id]], axis=0)
        value_rows = jnp.concatenate([root_values, seg_values[two_at], seg_values[one_at], seg_values[seg_id]], axis=0)
        key_mask = jnp.concatenate([jnp.ones((SEG_TOK, ROOT), bool), jnp.broadcast_to((positions < two_len)[None, :], (SEG_TOK, SEG_TOK)), jnp.broadcast_to((positions < one_len)[None, :], (SEG_TOK, SEG_TOK)), positions[None, :] <= positions[:, None]], axis=1)
        grad_rows = jnp.where((positions < own_len)[:, None], grad_out[seg_id], jnp.zeros((), jnp.bfloat16))
        grad_q, grad_k, grad_v = attend_back(queries[seg_id], attn_out[seg_id], grad_rows, key_rows, value_rows, key_mask)
        root_gk = root_gk + grad_k[:ROOT]
        root_gv = root_gv + grad_v[:ROOT]
        spans = ((two_at, ROOT), (one_at, ROOT + SEG_TOK), (seg_id, ROOT + 2 * SEG_TOK))
        for target, offset in spans:
            seg_gk = seg_gk.at[target].add(round_half(grad_k[offset:offset + SEG_TOK]))
            seg_gv = seg_gv.at[target].add(round_half(grad_v[offset:offset + SEG_TOK]))
        return ((root_gk, root_gv, seg_gk, seg_gv), grad_q.astype(jnp.bfloat16))
    start = (jnp.zeros((ROOT, width), jnp.float32), jnp.zeros((ROOT, width), jnp.float32), jnp.zeros((SEGS, SEG_TOK, width), jnp.float32), jnp.zeros((SEGS, SEG_TOK, width), jnp.float32))
    totals, grad_queries = lax.scan(segment_step, start, jnp.arange(SEGS, dtype=jnp.int32))
    root_gk, root_gv, seg_gk, seg_gv = totals
    return (grad_queries, seg_gk.astype(jnp.bfloat16), seg_gv.astype(jnp.bfloat16), root_gk.astype(jnp.bfloat16), root_gv.astype(jnp.bfloat16))
```

```python
import functools
import math

import jax
import jax.numpy as jnp
from jax import lax
from jax.experimental import pallas as pl
from jax.experimental.pallas import tpu as pltpu
from jax.sharding import PartitionSpec as P

HEADS = 32
KV_HEADS = 4
HEAD_DIM = 128
BLOCK = 128
GROUP = HEADS // KV_HEADS
SEG_TOK = 256
ROOT = 2048
CHUNK = 256
KEYS = ROOT + 3 * SEG_TOK
PER = 4
PIECES = 16
PIECE = SEG_TOK // PIECES
SCALE = 1.0 / math.sqrt(HEAD_DIM)
SCALE_LOG2 = SCALE * math.log2(math.e)
BF16 = jnp.bfloat16
F32 = jnp.float32


def dot(a, b):
    return lax.dot_general(a, b, (((1,), (0,)), ((), ())), preferred_element_type=F32)


def head_kernel(
    info, q_ref, g_ref, o_ref, mine_ref, other_ref, anc_ref, own_k_ref, own_v_ref,
    dq_ref, keep_ref, give_ref, anc_out_ref, own_out_ref,
    k_rows, k_cols, v_cols, s_buf, e_buf, ds_buf, q_cols, g_cols, acc_k, acc_v,
):
    rows = PER * SEG_TOK
    steps = GROUP // PER
    n_root = ROOT // CHUNK
    n_chunk = KEYS // CHUNK
    two_len, one_len, own_len, core = info[0], info[1], info[2], info[3]
    first_core = core == 0
    for j in range(n_chunk):
        span = slice(j * CHUNK, (j + 1) * CHUNK)
        if j < n_root:
            mine, other = mine_ref[span, :], other_ref[span, :]
            k_tile = jnp.where(first_core, mine, other)
            v_tile = jnp.where(first_core, other, mine)
        elif j < n_root + 2:
            k_tile = anc_ref[j - n_root, :, :HEAD_DIM]
            v_tile = anc_ref[j - n_root, :, HEAD_DIM:]
        else:
            k_tile, v_tile = own_k_ref[...], own_v_ref[...]
        k_rows[span, :] = k_tile
        k_cols[:, span] = k_tile.T
        v_cols[:, span] = v_tile.T

    def stack(ref, i):
        return jnp.concatenate(
            [ref[:, (i * PER + p) * HEAD_DIM : (i * PER + p + 1) * HEAD_DIM] for p in range(PER)],
            axis=0,
        )

    def row_ids():
        return lax.broadcasted_iota(jnp.int32, (rows, 1), 0) % SEG_TOK

    def scores(i):
        q = stack(q_ref, i)
        top = None
        for j in range(n_chunk):
            span = slice(j * CHUNK, (j + 1) * CHUNK)
            s = dot(q, k_cols[:, span])
            if j >= n_root:
                col = lax.broadcasted_iota(jnp.int32, (1, CHUNK), 1)
                if j == n_root:
                    live = col < two_len
                elif j == n_root + 1:
                    live = col < one_len
                else:
                    live = col <= row_ids()
                s = jnp.where(live, s, -jnp.inf)
            s_buf[i % 2, :, span] = s
            for w in range(0, CHUNK, 128):
                part = s[:, w : w + 128]
                top = part if top is None else jnp.maximum(top, part)
            yield None
        yield jnp.max(top, axis=-1, keepdims=True) * SCALE_LOG2

    def probs(i, top):
        g = jnp.where(row_ids() < own_len, stack(g_ref, i), jnp.zeros((), BF16))
        g_wide = g.astype(F32)
        delta = jnp.sum(g_wide * stack(o_ref, i).astype(F32), axis=-1, keepdims=True)
        dq = jnp.zeros((rows, HEAD_DIM), F32)
        total = None
        for j in range(n_chunk):
            span = slice(j * CHUNK, (j + 1) * CHUNK)
            e = jnp.exp2(s_buf[i % 2, :, span] * SCALE_LOG2 - top)
            for w in range(0, CHUNK, 128):
                part = e[:, w : w + 128]
                total = part if total is None else total + part
            e_buf[i % 2, :, span] = e.astype(BF16)
            dp = dot(g, v_cols[:, span])
            ds = (e * (dp - delta)).astype(BF16)
            ds_buf[i % 2, :, span] = ds
            dq = dq + dot(ds, k_rows[span, :])
            yield None
        inv = 1.0 / jnp.sum(total, axis=-1, keepdims=True)
        g_cols[i % 2] = (g_wide * inv).astype(BF16).T
        inv_scale = inv * SCALE
        q_cols[i % 2] = (stack(q_ref, i).astype(F32) * inv_scale).astype(BF16).T
        dq = dq * inv_scale
        for p in range(PER):
            at = (i * PER + p) * HEAD_DIM
            dq_ref[:, at : at + HEAD_DIM] = dq[p * SEG_TOK : (p + 1) * SEG_TOK].astype(BF16)
        yield None

    def keys(i):
        q, g = q_cols[i % 2], g_cols[i % 2]
        for j in range(n_chunk):
            span = slice(j * CHUNK, (j + 1) * CHUNK)
            dv = dot(g, e_buf[i % 2, :, span])
            dk = dot(q, ds_buf[i % 2, :, span])
            if i > 0:
                dv, dk = acc_v[:, span] + dv, acc_k[:, span] + dk
            if i < steps - 1:
                acc_v[:, span], acc_k[:, span] = dv, dk
            elif j < n_root:
                dk, dv = dk.astype(BF16), dv.astype(BF16)
                for w in range(0, CHUNK, 128):
                    block = (j * CHUNK + w) // 128
                    dk_tile, dv_tile = dk[:, w : w + 128], dv[:, w : w + 128]
                    keep_ref[block] = jnp.where(first_core, dk_tile, dv_tile)
                    give_ref[block] = jnp.where(first_core, dv_tile, dk_tile)
            else:
                dk, dv = dk.T.astype(BF16), dv.T.astype(BF16)
                if j < n_root + 2:
                    for p in range(PIECES):
                        piece = slice(p * PIECE, (p + 1) * PIECE)
                        anc_out_ref[p, j - n_root, :, :HEAD_DIM] = dk[piece]
                        anc_out_ref[p, j - n_root, :, HEAD_DIM:] = dv[piece]
                else:
                    own_out_ref[:, :HEAD_DIM] = dk
                    own_out_ref[:, HEAD_DIM:] = dv
            yield None
        yield None

    tops = {}
    for step in range(-1, steps + 1):
        running = []
        if step + 1 < steps:
            running.append((step + 1, scores(step + 1)))
        if 0 <= step < steps:
            running.append((None, probs(step, tops[step])))
        if 0 <= step - 1:
            running.append((None, keys(step - 1)))
        for _ in range(n_chunk + 1):
            for tag, stream in running:
                value = next(stream)
                if value is not None:
                    tops[tag] = value


def head_call(head, root_column, info, q, g, o, mine, other, anc, own_k, own_v):
    rows = PER * SEG_TOK
    wide = GROUP * HEAD_DIM

    def full(shape):
        return pl.BlockSpec(shape, lambda i: (0,) * len(shape))

    def columns(height, width, at):
        return pl.BlockSpec((height, width), lambda i: (0, at))

    shapes = ((SEG_TOK, wide), (16, 128, 128), (16, 128, 128), (PIECES, 2, PIECE, 256), (SEG_TOK, 256))
    return pl.pallas_call(
        head_kernel,
        grid=(1,),
        in_specs=[
            pl.BlockSpec(memory_space=pltpu.SMEM),
            columns(SEG_TOK, wide, head),
            columns(SEG_TOK, wide, head),
            columns(SEG_TOK, wide, head),
            columns(ROOT, HEAD_DIM, root_column),
            columns(ROOT, HEAD_DIM, root_column),
            full(anc.shape),
            columns(SEG_TOK, HEAD_DIM, head),
            columns(SEG_TOK, HEAD_DIM, head),
        ],
        out_specs=[full(s) for s in shapes],
        out_shape=[jax.ShapeDtypeStruct(s, BF16) for s in shapes],
        scratch_shapes=[
            pltpu.VMEM((KEYS, HEAD_DIM), BF16),
            pltpu.VMEM((HEAD_DIM, KEYS), BF16),
            pltpu.VMEM((HEAD_DIM, KEYS), BF16),
            pltpu.VMEM((2, rows, KEYS), F32),
            pltpu.VMEM((2, rows, KEYS), BF16),
            pltpu.VMEM((2, rows, KEYS), BF16),
            pltpu.VMEM((2, HEAD_DIM, rows), BF16),
            pltpu.VMEM((2, HEAD_DIM, rows), BF16),
            pltpu.VMEM((HEAD_DIM, KEYS), F32),
            pltpu.VMEM((HEAD_DIM, KEYS), F32),
        ],
        compiler_params=pltpu.CompilerParams(vmem_limit_bytes=60 * 2**20),
        cost_estimate=pl.CostEstimate(
            flops=5 * 2 * GROUP * SEG_TOK * KEYS * HEAD_DIM,
            bytes_accessed=6 * 2**20,
            transcendentals=GROUP * SEG_TOK * KEYS,
        ),
        name="head" + str(head),
    )(info, q, g, o, mine, other, anc, own_k, own_v)


def per_device(
    queries, attn_out, grad_out, seg_keys, seg_values, root_keys, root_values, parent, seg_blocks
):
    n_leaf = lax.axis_size("leaf")
    n_rep = lax.axis_size("rep")
    leaf_pos = lax.axis_index("leaf")
    rep_pos = lax.axis_index("rep")
    core = rep_pos % 2
    core_swap = [(r, r ^ 1) for r in range(n_rep)]

    def exchange(x):
        return lax.all_to_all(x, "leaf", 0, 0)

    def swap(x):
        return lax.ppermute(x, "rep", core_swap)

    row_parent = lax.dynamic_index_in_dim(parent.reshape(n_leaf, n_rep), rep_pos, 1, keepdims=False)
    row_blocks = lax.dynamic_index_in_dim(
        seg_blocks.reshape(n_leaf, n_rep), rep_pos, 1, keepdims=False
    )
    parent_one = row_parent
    parent_two = jnp.where(parent_one >= 0, row_parent[jnp.maximum(parent_one, 0)], -1)
    sources = jnp.stack([parent_two, parent_one], axis=1)
    lens = jnp.where(sources >= 0, row_blocks[jnp.maximum(sources, 0)] * BLOCK, 0)
    info = jnp.concatenate(
        [lens[leaf_pos], (row_blocks[leaf_pos] * BLOCK)[None], core[None].astype(jnp.int32)]
    )
    onehot = (jnp.arange(n_leaf)[:, None] == sources.reshape(1, -1)).astype(BF16)

    queries, attn_out, grad_out = queries[0], attn_out[0], grad_out[0]
    own_k, own_v = seg_keys[0], seg_values[0]

    root_mine = jnp.where(core == 0, root_keys, root_values)
    rest = lax.all_gather(root_mine[:, HEAD_DIM:], "leaf", axis=0, tiled=True)

    item = jnp.concatenate(
        [
            part[:, h * HEAD_DIM : (h + 1) * HEAD_DIM]
            for h in range(KV_HEADS)
            for part in (own_k, own_v)
        ],
        axis=1,
    ).reshape(PIECES, PIECE, KV_HEADS * 256)
    spread = exchange(item)
    first_mine = exchange(
        jnp.broadcast_to(root_mine[None, :, :HEAD_DIM], (n_leaf, root_mine.shape[0], HEAD_DIM))
    ).reshape(ROOT, HEAD_DIM)
    first_other = swap(first_mine)
    wanted = jnp.maximum(sources, 0)
    picked = spread[wanted]

    def ancestors(lo, hi):
        got = exchange(picked[..., lo * 256 : hi * 256])
        return jnp.moveaxis(got, 1, 0).reshape(2, SEG_TOK, (hi - lo) * 256)

    anc_first = ancestors(0, 1)
    anc_rest = ancestors(1, KV_HEADS)
    rest_other = swap(rest)

    dqs, plane, seg_k, seg_v = [], [], [], []
    for head in range(KV_HEADS):
        if head == 0:
            mine, other, anc, column = first_mine, first_other, anc_first, 0
        else:
            mine, other, column = rest, rest_other, head - 1
            anc = anc_rest[:, :, (head - 1) * 256 : head * 256]
        dq, keep, give, anc_terms, own_term = head_call(
            head, column, info, queries, grad_out, attn_out, mine, other, anc, own_k, own_v
        )
        dqs.append(dq)
        chip = (keep.astype(F32) + swap(give).astype(F32)).astype(BF16)
        plane.append(jnp.sum(exchange(chip).astype(F32), axis=0))
        terms = exchange(anc_terms).reshape(2 * n_leaf, PIECE * 256)
        sums = lax.dot_general(
            onehot, terms, (((1,), (0,)), ((), ())), preferred_element_type=F32
        ).astype(BF16)
        back = exchange(sums.reshape(n_leaf, PIECE, 256)).reshape(SEG_TOK, 256)
        seg = (back.astype(F32) + own_term.astype(F32)).astype(BF16)
        seg_k.append(seg[:, :HEAD_DIM])
        seg_v.append(seg[:, HEAD_DIM:])
    part = jnp.stack(plane)
    total = part
    for shift in (1, 2, 3):
        perm = [(r, (r + 2 * shift) % n_rep) for r in range(n_rep)]
        total = total + lax.ppermute(part, "rep", perm)
    total = jnp.moveaxis(total.astype(BF16), 2, 0).reshape(part.shape[2], KV_HEADS * HEAD_DIM)
    swapped = swap(total)
    return (
        jnp.concatenate(dqs, axis=1)[None],
        jnp.concatenate(seg_k, axis=1)[None],
        jnp.concatenate(seg_v, axis=1)[None],
        jnp.where(core == 0, total, swapped),
        jnp.where(core == 0, swapped, total),
    )


def solution(mesh):
    rows = P(("leaf", "rep"), None, None)
    root = P("leaf", None)
    return jax.shard_map(
        per_device,
        mesh=mesh,
        in_specs=(rows, rows, rows, rows, rows, root, root, P(), P()),
        out_specs=(rows, rows, rows, root, root),
        check_vma=False,
    )
```

```python
import functools
import math

import jax
import jax.numpy as jnp
from jax import lax
from jax.experimental import pallas as pl
from jax.experimental.pallas import tpu as pltpu
from jax.sharding import PartitionSpec as P

HEADS = 32
KV_HEADS = 4
HEAD_DIM = 128
BLOCK = 128
GROUP = HEADS // KV_HEADS
SEG_TOK = 256
ROOT = 2048
CHUNK = 256
KEYS = ROOT + 3 * SEG_TOK
PER = 4
PIECES = 16
PIECE = SEG_TOK // PIECES
TERM_ROWS = 4 * PIECE
SCALE = 1.0 / math.sqrt(HEAD_DIM)
SCALE_LOG2 = SCALE * math.log2(math.e)
BF16 = jnp.bfloat16
F32 = jnp.float32


def dot(a, b):
    return lax.dot_general(a, b, (((1,), (0,)), ((), ())), preferred_element_type=F32)


def head_kernel(
    info, q_ref, g_ref, o_ref, mine_ref, other_ref, anc_ref, own_k_ref, own_v_ref,
    dq_ref, keep_ref, give_ref, anc_out_ref, own_out_ref,
    k_rows, k_cols, v_cols, s_buf, e_buf, ds_buf, q_cols, g_cols, acc_k, acc_v,
):
    rows = PER * SEG_TOK
    steps = GROUP // PER
    n_root = ROOT // CHUNK
    n_chunk = KEYS // CHUNK
    two_len, one_len, own_len, core = info[0], info[1], info[2], info[3]
    first_core = core == 0

    def load_root(ref, j):
        if len(ref.shape) == 2:
            return ref[j * CHUNK : (j + 1) * CHUNK, :]
        per = CHUNK // ref.shape[1]
        return jnp.concatenate([ref[j * per + b] for b in range(per)], axis=0)

    for j in range(n_chunk):
        span = slice(j * CHUNK, (j + 1) * CHUNK)
        if j < n_root:
            mine, other = load_root(mine_ref, j), load_root(other_ref, j)
            k_tile = jnp.where(first_core, mine, other)
            v_tile = jnp.where(first_core, other, mine)
        elif j < n_root + 2:
            k_at, v_at = (j - n_root) * 2 * PIECE, ((j - n_root) * 2 + 1) * PIECE
            k_tile = jnp.concatenate([anc_ref[p, k_at : k_at + PIECE] for p in range(PIECES)], axis=0)
            v_tile = jnp.concatenate([anc_ref[p, v_at : v_at + PIECE] for p in range(PIECES)], axis=0)
        else:
            k_tile, v_tile = own_k_ref[...], own_v_ref[...]
        k_rows[span, :] = k_tile
        k_cols[:, span] = k_tile.T
        v_cols[:, span] = v_tile.T

    def stack(ref, i):
        return jnp.concatenate(
            [ref[:, (i * PER + p) * HEAD_DIM : (i * PER + p + 1) * HEAD_DIM] for p in range(PER)],
            axis=0,
        )

    def row_ids():
        return lax.broadcasted_iota(jnp.int32, (rows, 1), 0) % SEG_TOK

    def scores(i):
        q = stack(q_ref, i)
        top = None
        for j in range(n_chunk):
            span = slice(j * CHUNK, (j + 1) * CHUNK)
            s = dot(q, k_cols[:, span])
            if j >= n_root:
                col = lax.broadcasted_iota(jnp.int32, (1, CHUNK), 1)
                if j == n_root:
                    live = col < two_len
                elif j == n_root + 1:
                    live = col < one_len
                else:
                    live = col <= row_ids()
                s = jnp.where(live, s, -jnp.inf)
            s_buf[i % 2, :, span] = s
            for w in range(0, CHUNK, 128):
                part = s[:, w : w + 128]
                top = part if top is None else jnp.maximum(top, part)
            yield None
        yield jnp.max(top, axis=-1, keepdims=True) * SCALE_LOG2

    def probs(i, top):
        g = jnp.where(row_ids() < own_len, stack(g_ref, i), jnp.zeros((), BF16))
        g_wide = g.astype(F32)
        delta = jnp.sum(g_wide * stack(o_ref, i).astype(F32), axis=-1, keepdims=True)
        dq = jnp.zeros((rows, HEAD_DIM), F32)
        total = None
        for j in range(n_chunk):
            span = slice(j * CHUNK, (j + 1) * CHUNK)
            e = jnp.exp2(s_buf[i % 2, :, span] * SCALE_LOG2 - top)
            for w in range(0, CHUNK, 128):
                part = e[:, w : w + 128]
                total = part if total is None else total + part
            e_buf[i % 2, :, span] = e.astype(BF16)
            dp = dot(g, v_cols[:, span])
            ds = (e * (dp - delta)).astype(BF16)
            ds_buf[i % 2, :, span] = ds
            dq = dq + dot(ds, k_rows[span, :])
            yield None
        inv = 1.0 / jnp.sum(total, axis=-1, keepdims=True)
        g_cols[i % 2] = (g_wide * inv).astype(BF16).T
        inv_scale = inv * SCALE
        q_cols[i % 2] = (stack(q_ref, i).astype(F32) * inv_scale).astype(BF16).T
        dq = dq * inv_scale
        for p in range(PER):
            at = (i * PER + p) * HEAD_DIM
            dq_ref[:, at : at + HEAD_DIM] = dq[p * SEG_TOK : (p + 1) * SEG_TOK].astype(BF16)
        yield None

    def keys(i):
        q, g = q_cols[i % 2], g_cols[i % 2]
        for j in range(n_chunk):
            span = slice(j * CHUNK, (j + 1) * CHUNK)
            dv = dot(g, e_buf[i % 2, :, span])
            dk = dot(q, ds_buf[i % 2, :, span])
            if i > 0:
                dv, dk = acc_v[:, span] + dv, acc_k[:, span] + dk
            if i < steps - 1:
                acc_v[:, span], acc_k[:, span] = dv, dk
            elif j < n_root:
                dk, dv = dk.astype(BF16), dv.astype(BF16)
                for w in range(0, CHUNK, 128):
                    block = (j * CHUNK + w) // 128
                    dk_tile, dv_tile = dk[:, w : w + 128], dv[:, w : w + 128]
                    keep_ref[block] = jnp.where(first_core, dk_tile, dv_tile)
                    give_ref[block] = jnp.where(first_core, dv_tile, dk_tile)
            else:
                dk, dv = dk.T.astype(BF16), dv.T.astype(BF16)
                if j < n_root + 2:
                    k_at, v_at = (j - n_root) * 2 * PIECE, ((j - n_root) * 2 + 1) * PIECE
                    for p in range(PIECES):
                        piece = slice(p * PIECE, (p + 1) * PIECE)
                        anc_out_ref[p, k_at : k_at + PIECE] = dk[piece]
                        anc_out_ref[p, v_at : v_at + PIECE] = dv[piece]
                else:
                    own_out_ref[:, :HEAD_DIM] = dk
                    own_out_ref[:, HEAD_DIM:] = dv
            yield None
        yield None

    tops = {}
    for step in range(-1, steps + 1):
        running = []
        if step + 1 < steps:
            running.append((step + 1, scores(step + 1)))
        if 0 <= step < steps:
            running.append((None, probs(step, tops[step])))
        if 0 <= step - 1:
            running.append((None, keys(step - 1)))
        for _ in range(n_chunk + 1):
            for tag, stream in running:
                value = next(stream)
                if value is not None:
                    tops[tag] = value


def head_call(head, root_column, anc_block, info, q, g, o, mine, other, anc, own_k, own_v):
    rows = PER * SEG_TOK
    wide = GROUP * HEAD_DIM

    def full(shape):
        return pl.BlockSpec(shape, lambda i: (0,) * len(shape))

    def columns(height, width, at):
        return pl.BlockSpec((height, width), lambda i: (0, at))

    def root_spec(x):
        return full(x.shape) if x.ndim == 3 else columns(ROOT, HEAD_DIM, root_column)

    shapes = (
        (SEG_TOK, wide), (16, 128, 128), (16, 128, 128), (PIECES, TERM_ROWS, 128), (SEG_TOK, 256)
    )
    return pl.pallas_call(
        head_kernel,
        grid=(1,),
        in_specs=[
            pl.BlockSpec(memory_space=pltpu.SMEM),
            columns(SEG_TOK, wide, head),
            columns(SEG_TOK, wide, head),
            columns(SEG_TOK, wide, head),
            root_spec(mine),
            root_spec(other),
            pl.BlockSpec((PIECES, TERM_ROWS, 128), lambda i: (0, anc_block, 0)),
            columns(SEG_TOK, HEAD_DIM, head),
            columns(SEG_TOK, HEAD_DIM, head),
        ],
        out_specs=[full(s) for s in shapes],
        out_shape=[jax.ShapeDtypeStruct(s, BF16) for s in shapes],
        scratch_shapes=[
            pltpu.VMEM((KEYS, HEAD_DIM), BF16),
            pltpu.VMEM((HEAD_DIM, KEYS), BF16),
            pltpu.VMEM((HEAD_DIM, KEYS), BF16),
            pltpu.VMEM((2, rows, KEYS), F32),
            pltpu.VMEM((2, rows, KEYS), BF16),
            pltpu.VMEM((2, rows, KEYS), BF16),
            pltpu.VMEM((2, HEAD_DIM, rows), BF16),
            pltpu.VMEM((2, HEAD_DIM, rows), BF16),
            pltpu.VMEM((HEAD_DIM, KEYS), F32),
            pltpu.VMEM((HEAD_DIM, KEYS), F32),
        ],
        compiler_params=pltpu.CompilerParams(vmem_limit_bytes=60 * 2**20),
        cost_estimate=pl.CostEstimate(
            flops=5 * 2 * GROUP * SEG_TOK * KEYS * HEAD_DIM,
            bytes_accessed=50 * 2**20,
            transcendentals=GROUP * SEG_TOK * KEYS,
        ),
        name="head" + str(head),
    )(info, q, g, o, mine, other, anc, own_k, own_v)


def small_call(kernel, shapes, name, *args, scratch=()):
    vmem = pl.BlockSpec(memory_space=pltpu.VMEM)
    smem = pl.BlockSpec(memory_space=pltpu.SMEM)
    return pl.pallas_call(
        kernel,
        in_specs=[smem if a.dtype == jnp.int32 else vmem for a in args],
        out_specs=[vmem] * len(shapes),
        out_shape=[jax.ShapeDtypeStruct(s, BF16) for s in shapes],
        scratch_shapes=scratch,
        compiler_params=pltpu.CompilerParams(vmem_limit_bytes=32 * 2**20),
        cost_estimate=pl.CostEstimate(flops=10**6, bytes_accessed=3 * 2**20, transcendentals=0),
        name=name,
    )(*args)


def front_kernel(info, root_k, root_v, own_k, own_v, send, rest):
    first_core = info[3] == 0
    mine = jnp.where(first_core, root_k[...], root_v[...])
    rest[...] = mine[:, HEAD_DIM:]
    for p in range(PIECES):
        send[p, :128] = mine[:, :HEAD_DIM]
        piece = slice(p * PIECE, (p + 1) * PIECE)
        for h in range(KV_HEADS):
            for c, part in enumerate((own_k, own_v)):
                at = 128 + (2 * h + c) * PIECE
                send[p, at : at + PIECE] = part[piece, h * HEAD_DIM : (h + 1) * HEAD_DIM]


def forward_kernel(wanted, got, rest, mine, send_first, send_rest):
    for p in range(PIECES):
        mine[p] = got[p, :128]
        send_rest[p, 3 * TERM_ROWS :] = rest[:, :HEAD_DIM]
        for w in range(2):
            source = wanted[2 * p + w]
            for h in range(KV_HEADS):
                rows = got[source, 128 + h * 2 * PIECE : 128 + (h + 1) * 2 * PIECE]
                if h == 0:
                    send_first[p, w * 2 * PIECE : (w + 1) * 2 * PIECE] = rows
                else:
                    at = (h - 1) * TERM_ROWS + w * 2 * PIECE
                    send_rest[p, at : at + 2 * PIECE] = rows


def pack_kernel(n_root, n_terms, *refs):
    out = refs[-1]
    for i in range(n_root):
        keep, got = refs[2 * i], refs[2 * i + 1]
        for b in range(16):
            total = keep[b].astype(F32) + got[b].astype(F32)
            out[b, i * 128 : (i + 1) * 128] = total.astype(BF16)
    for i in range(n_terms):
        at = n_root * 128 + i * TERM_ROWS
        out[:, at : at + TERM_ROWS] = refs[2 * n_root + i][...]


def pack(roots, terms, name):
    n_root, n_terms = len(roots), len(terms)
    rows = n_root * 128 + n_terms * TERM_ROWS
    flat = [x for pair in roots for x in pair] + list(terms)
    return small_call(
        functools.partial(pack_kernel, n_root, n_terms), [(16, rows, 128)], name, *flat
    )[0]


def reduce_kernel(n_root, n_terms, n_before, sources, got, *refs):
    before, planes, sums, acc = refs[:n_before], refs[n_before], refs[n_before + 1], refs[-1]
    for i in range(n_root):
        total = got[0, i * 128 : (i + 1) * 128].astype(F32)
        for d in range(1, 16):
            total += got[d, i * 128 : (i + 1) * 128].astype(F32)
        planes[i] = total.astype(BF16)
    acc[...] = jnp.zeros_like(acc)
    for d in range(16):
        for w in range(2):
            target = sources[2 * d + w]

            @pl.when(target >= 0)
            def _():
                for i in range(n_terms):
                    at = n_root * 128 + i * TERM_ROWS + w * 2 * PIECE
                    rows = slice(i * 2 * PIECE, (i + 1) * 2 * PIECE)
                    acc[target, rows] += got[d, at : at + 2 * PIECE].astype(F32)

    at = 0
    for ref in before:
        height = ref.shape[1]
        sums[:, at : at + height] = ref[...]
        at += height
    sums[:, at:] = acc[...].astype(BF16)


def reduce_parts(n_root, n_terms, sources, got, before, name):
    rows = n_terms * 2 * PIECE + sum(b.shape[1] for b in before)
    return small_call(
        functools.partial(reduce_kernel, n_root, n_terms, len(before)),
        [(n_root, 128, 128), (16, rows, 128)],
        name, sources, got, *before,
        scratch=[pltpu.VMEM((16, n_terms * 2 * PIECE, 128), F32)],
    )


def finish_seg_kernel(back, *refs):
    own, out_k, out_v = refs[:-2], refs[-2], refs[-1]
    for h in range(KV_HEADS):
        cols = slice(h * HEAD_DIM, (h + 1) * HEAD_DIM)
        for p in range(PIECES):
            piece = slice(p * PIECE, (p + 1) * PIECE)
            for c, out in enumerate((out_k, out_v)):
                at = (2 * h + c) * PIECE
                term = own[h][piece, c * HEAD_DIM : (c + 1) * HEAD_DIM]
                total = back[p, at : at + PIECE].astype(F32) + term.astype(F32)
                out[piece, cols] = total.astype(BF16)


def finish_root_kernel(*refs):
    out = refs[-1]
    for h in range(KV_HEADS):
        total = refs[0][h].astype(F32)
        for ref in refs[1:-1]:
            total += ref[h].astype(F32)
        out[:, h * HEAD_DIM : (h + 1) * HEAD_DIM] = total.T.astype(BF16)


def after(x, *deps):
    return lax.optimization_barrier((x,) + deps)[0]


def per_device(
    queries, attn_out, grad_out, seg_keys, seg_values, root_keys, root_values, parent, seg_blocks
):
    n_leaf = lax.axis_size("leaf")
    n_rep = lax.axis_size("rep")
    leaf_pos = lax.axis_index("leaf")
    rep_pos = lax.axis_index("rep")
    core = rep_pos % 2
    core_swap = [(r, r ^ 1) for r in range(n_rep)]

    def exchange(x):
        return lax.all_to_all(x, "leaf", 0, 0)

    def swap(x):
        return lax.ppermute(x, "rep", core_swap)

    row_parent = lax.dynamic_index_in_dim(parent.reshape(n_leaf, n_rep), rep_pos, 1, keepdims=False)
    row_blocks = lax.dynamic_index_in_dim(
        seg_blocks.reshape(n_leaf, n_rep), rep_pos, 1, keepdims=False
    )
    parent_two = jnp.where(row_parent >= 0, row_parent[jnp.maximum(row_parent, 0)], -1)
    sources = jnp.stack([parent_two, row_parent], axis=1)
    lens = jnp.where(sources >= 0, row_blocks[jnp.maximum(sources, 0)] * BLOCK, 0)
    info = jnp.concatenate(
        [lens[leaf_pos], (row_blocks[leaf_pos] * BLOCK)[None], core[None].astype(jnp.int32)]
    )
    sources = sources.reshape(-1)

    queries, attn_out, grad_out = queries[0], attn_out[0], grad_out[0]
    own_k, own_v = seg_keys[0], seg_values[0]

    core_info = jnp.concatenate([jnp.zeros((3,), jnp.int32), core[None].astype(jnp.int32)])
    send, rest = small_call(
        front_kernel, [(16, 256, 128), (128, 384)], "front",
        core_info, root_keys, root_values, own_k, own_v,
    )
    last_mine = lax.all_gather(rest[:, HEAD_DIM:], "leaf", axis=0, tiled=True)
    got = exchange(send)
    mine_0, send_first, send_rest = small_call(
        forward_kernel, [(16, 128, 128), (16, TERM_ROWS, 128), (16, 3 * TERM_ROWS + 128, 128)],
        "forward", jnp.maximum(sources, 0), got, rest,
    )
    other_0 = swap(mine_0)
    anc_0 = exchange(send_first)
    got_rest = exchange(send_rest)

    def run(head, column, anc_block, info, mine, other, anc):
        return head_call(
            head, column, anc_block, info, queries, grad_out, attn_out, mine, other, anc, own_k, own_v
        )

    info_0 = after(info, send_rest, anc_0)
    dq_0, keep_0, give_0, terms_0, own_0 = run(0, 0, 0, info_0, mine_0, other_0, anc_0)

    got_rest = after(got_rest, dq_0)
    mine_1 = got_rest[:, 3 * TERM_ROWS :]
    other_1 = swap(mine_1)
    info_1 = after(info, give_0)
    dq_1, keep_1, give_1, terms_1, own_1 = run(1, 0, 0, info_1, mine_1, other_1, got_rest)

    last_other = swap(after(last_mine, dq_0))
    got_0 = after(swap(give_0), dq_1)
    send_a = pack([(keep_0, got_0)], [terms_0, terms_1], "pack_a")
    info_2 = after(info, send_a)
    dq_2, keep_2, give_2, terms_2, own_2 = run(2, 0, 1, info_2, last_mine, last_other, got_rest)

    back_a = after(exchange(send_a), dq_2)
    got_1 = after(swap(give_1), dq_2)
    send_b = pack([(keep_1, got_1)], [terms_2], "pack_b")
    info_3 = after(info, send_b)
    dq_3, keep_3, give_3, terms_3, own_3 = run(3, 1, 2, info_3, last_mine, last_other, got_rest)

    back_b = after(exchange(send_b), dq_3)
    got_2 = after(swap(give_2), dq_3)
    send_c = pack([(keep_2, got_2), (keep_3, swap(give_3))], [terms_3], "pack_c")
    back_a, back_b = after(back_a, send_c), after(back_b, send_c)
    plane_a, sums_a = reduce_parts(1, 2, sources, back_a, (), "reduce_a")
    plane_b, sums_b = reduce_parts(1, 1, sources, back_b, (), "reduce_b")
    plane_c, sums = reduce_parts(2, 1, sources, exchange(send_c), (sums_a, sums_b), "reduce_c")
    back = exchange(sums)
    part = jnp.concatenate([plane_a, plane_b, plane_c], axis=0)
    shifted = []
    for shift in (1, 2, 3):
        perm = [(r, (r + 2 * shift) % n_rep) for r in range(n_rep)]
        shifted.append(lax.ppermute(part, "rep", perm))
    total = small_call(finish_root_kernel, [(128, 512)], "finish_root", part, *shifted)[0]
    swapped = swap(total)
    seg_k, seg_v = small_call(
        finish_seg_kernel, [(SEG_TOK, 512)] * 2, "finish_seg", back, own_0, own_1, own_2, own_3
    )
    return (
        jnp.concatenate([dq_0, dq_1, dq_2, dq_3], axis=1)[None],
        seg_k[None],
        seg_v[None],
        jnp.where(core == 0, total, swapped),
        jnp.where(core == 0, swapped, total),
    )


def solution(mesh):
    rows = P(("leaf", "rep"), None, None)
    root = P("leaf", None)
    return jax.shard_map(
        per_device,
        mesh=mesh,
        in_specs=(rows, rows, rows, rows, rows, root, root, P(), P()),
        out_specs=(rows, rows, rows, root, root),
        check_vma=False,
    )
```

```python
import functools
import math

import jax
import jax.numpy as jnp
from jax import lax
from jax.experimental import pallas as pl
from jax.experimental.pallas import tpu as pltpu
from jax.sharding import PartitionSpec as P

HEADS = 32
KV_HEADS = 4
HEAD_DIM = 128
BLOCK = 128
GROUP = HEADS // KV_HEADS
SEG_TOK = 256
ROOT = 2048
CHUNK = 256
KEYS = ROOT + 3 * SEG_TOK
PER = 2
PIECES = 16
PIECE = SEG_TOK // PIECES
TERM_ROWS = 4 * PIECE
SCALE = 1.0 / math.sqrt(HEAD_DIM)
SCALE_LOG2 = SCALE * math.log2(math.e)
BF16 = jnp.bfloat16
F32 = jnp.float32


def dot(a, b):
    return lax.dot_general(a, b, (((1,), (0,)), ((), ())), preferred_element_type=F32)


def head_kernel(
    info, q_ref, g_ref, o_ref, mine_ref, other_ref, anc_ref, own_k_ref, own_v_ref,
    dq_ref, keep_ref, give_ref, anc_out_ref, own_out_ref,
    k_rows, k_cols, v_cols, s_buf, e_buf, ds_buf, q_cols, g_cols, acc_k, acc_v,
):
    rows = PER * SEG_TOK
    steps = GROUP // PER
    n_root = ROOT // CHUNK
    n_chunk = KEYS // CHUNK
    two_len, one_len, own_len, core = info[0], info[1], info[2], info[3]
    first_core = core == 0

    def load_root(ref, j):
        if len(ref.shape) == 2:
            return ref[j * CHUNK : (j + 1) * CHUNK, :]
        per = CHUNK // ref.shape[1]
        return jnp.concatenate([ref[j * per + b] for b in range(per)], axis=0)

    for j in range(n_chunk):
        span = slice(j * CHUNK, (j + 1) * CHUNK)
        if j < n_root:
            mine, other = load_root(mine_ref, j), load_root(other_ref, j)
            k_tile = jnp.where(first_core, mine, other)
            v_tile = jnp.where(first_core, other, mine)
        elif j < n_root + 2:
            k_at, v_at = (j - n_root) * 2 * PIECE, ((j - n_root) * 2 + 1) * PIECE
            k_tile = jnp.concatenate([anc_ref[p, k_at : k_at + PIECE] for p in range(PIECES)], axis=0)
            v_tile = jnp.concatenate([anc_ref[p, v_at : v_at + PIECE] for p in range(PIECES)], axis=0)
        else:
            k_tile, v_tile = own_k_ref[...], own_v_ref[...]
        k_rows[span, :] = k_tile
        k_cols[:, span] = k_tile.T
        v_cols[:, span] = v_tile.T

    def stack(ref, i):
        return jnp.concatenate(
            [ref[:, (i * PER + p) * HEAD_DIM : (i * PER + p + 1) * HEAD_DIM] for p in range(PER)],
            axis=0,
        )

    def row_ids():
        return lax.broadcasted_iota(jnp.int32, (rows, 1), 0) % SEG_TOK

    def scores(i):
        q = stack(q_ref, i)
        top = None
        for j in range(n_chunk):
            span = slice(j * CHUNK, (j + 1) * CHUNK)
            s = dot(q, k_cols[:, span])
            if j >= n_root:
                col = lax.broadcasted_iota(jnp.int32, (1, CHUNK), 1)
                if j == n_root:
                    live = col < two_len
                elif j == n_root + 1:
                    live = col < one_len
                else:
                    live = col <= row_ids()
                s = jnp.where(live, s, -jnp.inf)
            s_buf[i % 2, :, span] = s
            for w in range(0, CHUNK, 128):
                part = s[:, w : w + 128]
                top = part if top is None else jnp.maximum(top, part)
            yield None
        yield jnp.max(top, axis=-1, keepdims=True) * SCALE_LOG2

    def probs(i, top):
        g = jnp.where(row_ids() < own_len, stack(g_ref, i), jnp.zeros((), BF16))
        g_wide = g.astype(F32)
        delta = jnp.sum(g_wide * stack(o_ref, i).astype(F32), axis=-1, keepdims=True)
        dq = jnp.zeros((rows, HEAD_DIM), F32)
        total = None
        for j in range(n_chunk):
            span = slice(j * CHUNK, (j + 1) * CHUNK)
            e = jnp.exp2(s_buf[i % 2, :, span] * SCALE_LOG2 - top)
            for w in range(0, CHUNK, 128):
                part = e[:, w : w + 128]
                total = part if total is None else total + part
            e_buf[i % 2, :, span] = e.astype(BF16)
            dp = dot(g, v_cols[:, span])
            ds = (e * (dp - delta)).astype(BF16)
            ds_buf[i % 2, :, span] = ds
            dq = dq + dot(ds, k_rows[span, :])
            yield None
        inv = 1.0 / jnp.sum(total, axis=-1, keepdims=True)
        g_cols[i % 2] = (g_wide * inv).astype(BF16).T
        inv_scale = inv * SCALE
        q_cols[i % 2] = (stack(q_ref, i).astype(F32) * inv_scale).astype(BF16).T
        dq = dq * inv_scale
        for p in range(PER):
            at = (i * PER + p) * HEAD_DIM
            dq_ref[:, at : at + HEAD_DIM] = dq[p * SEG_TOK : (p + 1) * SEG_TOK].astype(BF16)
        yield None

    def keys(i):
        q, g = q_cols[i % 2], g_cols[i % 2]
        for j in range(n_chunk):
            span = slice(j * CHUNK, (j + 1) * CHUNK)
            dv = dot(g, e_buf[i % 2, :, span])
            dk = dot(q, ds_buf[i % 2, :, span])
            if i > 0:
                dv, dk = acc_v[:, span] + dv, acc_k[:, span] + dk
            if i < steps - 1:
                acc_v[:, span], acc_k[:, span] = dv, dk
            elif j < n_root:
                dk, dv = dk.astype(BF16), dv.astype(BF16)
                for w in range(0, CHUNK, 128):
                    block = (j * CHUNK + w) // 128
                    dk_tile, dv_tile = dk[:, w : w + 128], dv[:, w : w + 128]
                    keep_ref[block] = jnp.where(first_core, dk_tile, dv_tile)
                    give_ref[block] = jnp.where(first_core, dv_tile, dk_tile)
            else:
                dk, dv = dk.T.astype(BF16), dv.T.astype(BF16)
                if j < n_root + 2:
                    k_at, v_at = (j - n_root) * 2 * PIECE, ((j - n_root) * 2 + 1) * PIECE
                    for p in range(PIECES):
                        piece = slice(p * PIECE, (p + 1) * PIECE)
                        anc_out_ref[p, k_at : k_at + PIECE] = dk[piece]
                        anc_out_ref[p, v_at : v_at + PIECE] = dv[piece]
                else:
                    own_out_ref[:, :HEAD_DIM] = dk
                    own_out_ref[:, HEAD_DIM:] = dv
            yield None
        yield None

    tops = {}
    for step in range(-1, steps + 1):
        running = []
        if step + 1 < steps:
            running.append((step + 1, scores(step + 1)))
        if 0 <= step < steps:
            running.append((None, probs(step, tops[step])))
        if 0 <= step - 1:
            running.append((None, keys(step - 1)))
        for _ in range(n_chunk + 1):
            for tag, stream in running:
                value = next(stream)
                if value is not None:
                    tops[tag] = value


def head_call(head, root_column, anc_block, info, q, g, o, mine, other, anc, own_k, own_v):
    rows = PER * SEG_TOK
    wide = GROUP * HEAD_DIM

    def full(shape):
        return pl.BlockSpec(shape, lambda i: (0,) * len(shape))

    def columns(height, width, at):
        return pl.BlockSpec((height, width), lambda i: (0, at))

    def root_spec(x):
        return full(x.shape) if x.ndim == 3 else columns(ROOT, HEAD_DIM, root_column)

    shapes = (
        (SEG_TOK, wide), (16, 128, 128), (16, 128, 128), (PIECES, TERM_ROWS, 128), (SEG_TOK, 256)
    )
    return pl.pallas_call(
        head_kernel,
        grid=(1,),
        in_specs=[
            pl.BlockSpec(memory_space=pltpu.SMEM),
            columns(SEG_TOK, wide, head),
            columns(SEG_TOK, wide, head),
            columns(SEG_TOK, wide, head),
            root_spec(mine),
            root_spec(other),
            pl.BlockSpec((PIECES, TERM_ROWS, 128), lambda i: (0, anc_block, 0)),
            columns(SEG_TOK, HEAD_DIM, head),
            columns(SEG_TOK, HEAD_DIM, head),
        ],
        out_specs=[full(s) for s in shapes],
        out_shape=[jax.ShapeDtypeStruct(s, BF16) for s in shapes],
        scratch_shapes=[
            pltpu.VMEM((KEYS, HEAD_DIM), BF16),
            pltpu.VMEM((HEAD_DIM, KEYS), BF16),
            pltpu.VMEM((HEAD_DIM, KEYS), BF16),
            pltpu.VMEM((2, rows, KEYS), F32),
            pltpu.VMEM((2, rows, KEYS), BF16),
            pltpu.VMEM((2, rows, KEYS), BF16),
            pltpu.VMEM((2, HEAD_DIM, rows), BF16),
            pltpu.VMEM((2, HEAD_DIM, rows), BF16),
            pltpu.VMEM((HEAD_DIM, KEYS), F32),
            pltpu.VMEM((HEAD_DIM, KEYS), F32),
        ],
        compiler_params=pltpu.CompilerParams(vmem_limit_bytes=60 * 2**20),
        cost_estimate=pl.CostEstimate(
            flops=5 * 2 * GROUP * SEG_TOK * KEYS * HEAD_DIM,
            bytes_accessed=50 * 2**20,
            transcendentals=GROUP * SEG_TOK * KEYS,
        ),
        name="head" + str(head),
    )(info, q, g, o, mine, other, anc, own_k, own_v)


def small_call(kernel, shapes, name, *args, scratch=(), from_hbm=False):
    smem = pl.BlockSpec(memory_space=pltpu.SMEM)
    vmem = pl.BlockSpec(memory_space=pltpu.VMEM)

    def spec(shape):
        return pl.BlockSpec(shape, lambda *i: (0,) * len(shape)) if from_hbm else vmem

    return pl.pallas_call(
        kernel,
        grid=(1,) if from_hbm else (),
        in_specs=[smem if a.dtype == jnp.int32 else spec(a.shape) for a in args],
        out_specs=[spec(s) for s in shapes],
        out_shape=[jax.ShapeDtypeStruct(s, BF16) for s in shapes],
        scratch_shapes=scratch,
        compiler_params=pltpu.CompilerParams(vmem_limit_bytes=(60 if from_hbm else 16) * 2**20),
        cost_estimate=pl.CostEstimate(flops=10**6, bytes_accessed=3 * 2**20, transcendentals=0),
        name=name,
    )(*args)


def front_kernel(info, root_k, root_v, own_k, own_v, send, rest):
    first_core = info[3] == 0
    mine = jnp.where(first_core, root_k[...], root_v[...])
    rest[...] = mine[:, HEAD_DIM:]
    for p in range(PIECES):
        send[p, :128] = mine[:, :HEAD_DIM]
        piece = slice(p * PIECE, (p + 1) * PIECE)
        for h in range(KV_HEADS):
            for c, part in enumerate((own_k, own_v)):
                at = 128 + (2 * h + c) * PIECE
                send[p, at : at + PIECE] = part[piece, h * HEAD_DIM : (h + 1) * HEAD_DIM]


def forward_kernel(wanted, got, rest, mine, send_first, send_rest):
    for p in range(PIECES):
        mine[p] = got[p, :128]
        send_rest[p, 3 * TERM_ROWS :] = rest[:, :HEAD_DIM]
        for w in range(2):
            source = wanted[2 * p + w]
            for h in range(KV_HEADS):
                rows = got[source, 128 + h * 2 * PIECE : 128 + (h + 1) * 2 * PIECE]
                if h == 0:
                    send_first[p, w * 2 * PIECE : (w + 1) * 2 * PIECE] = rows
                else:
                    at = (h - 1) * TERM_ROWS + w * 2 * PIECE
                    send_rest[p, at : at + 2 * PIECE] = rows


def pack_kernel(n_root, n_terms, *refs):
    out = refs[-1]
    for i in range(n_root):
        keep, got = refs[2 * i], refs[2 * i + 1]
        for b in range(16):
            total = keep[b].astype(F32) + got[b].astype(F32)
            out[b, i * 128 : (i + 1) * 128] = total.astype(BF16)
    for i in range(n_terms):
        at = n_root * 128 + i * TERM_ROWS
        out[:, at : at + TERM_ROWS] = refs[2 * n_root + i][...]


def pack(roots, terms, name):
    n_root, n_terms = len(roots), len(terms)
    rows = n_root * 128 + n_terms * TERM_ROWS
    flat = [x for pair in roots for x in pair] + list(terms)
    return small_call(
        functools.partial(pack_kernel, n_root, n_terms), [(16, rows, 128)], name, *flat
    )[0]


def reduce_kernel(n_root, n_terms, n_before, sources, got, *refs):
    before, planes, sums, acc = refs[:n_before], refs[n_before], refs[n_before + 1], refs[-1]
    for i in range(n_root):
        total = got[0, i * 128 : (i + 1) * 128].astype(F32)
        for d in range(1, 16):
            total += got[d, i * 128 : (i + 1) * 128].astype(F32)
        planes[i] = total.astype(BF16)
    acc[...] = jnp.zeros_like(acc)
    for d in range(16):
        for w in range(2):
            target = sources[2 * d + w]

            @pl.when(target >= 0)
            def _():
                for i in range(n_terms):
                    at = n_root * 128 + i * TERM_ROWS + w * 2 * PIECE
                    rows = slice(i * 2 * PIECE, (i + 1) * 2 * PIECE)
                    acc[target, rows] += got[d, at : at + 2 * PIECE].astype(F32)

    at = 0
    for ref in before:
        height = ref.shape[1]
        sums[:, at : at + height] = ref[...]
        at += height
    sums[:, at:] = acc[...].astype(BF16)


def reduce_parts(n_root, n_terms, sources, got, before, name):
    rows = n_terms * 2 * PIECE + sum(b.shape[1] for b in before)
    return small_call(
        functools.partial(reduce_kernel, n_root, n_terms, len(before)),
        [(n_root, 128, 128), (16, rows, 128)],
        name, sources, got, *before,
        scratch=[pltpu.VMEM((16, n_terms * 2 * PIECE, 128), F32)],
    )


def finish_seg_kernel(back, *refs):
    own, out_k, out_v = refs[:-2], refs[-2], refs[-1]
    for h in range(KV_HEADS):
        cols = slice(h * HEAD_DIM, (h + 1) * HEAD_DIM)
        for p in range(PIECES):
            piece = slice(p * PIECE, (p + 1) * PIECE)
            for c, out in enumerate((out_k, out_v)):
                at = (2 * h + c) * PIECE
                term = own[h][piece, c * HEAD_DIM : (c + 1) * HEAD_DIM]
                total = back[p, at : at + PIECE].astype(F32) + term.astype(F32)
                out[piece, cols] = total.astype(BF16)


def finish_root_kernel(*refs):
    out = refs[-1]
    for h in range(KV_HEADS):
        total = refs[0][h].astype(F32)
        for ref in refs[1:-1]:
            total += ref[h].astype(F32)
        out[:, h * HEAD_DIM : (h + 1) * HEAD_DIM] = total.T.astype(BF16)


def after(x, *deps):
    return lax.optimization_barrier((x,) + deps)[0]


def per_device(
    queries, attn_out, grad_out, seg_keys, seg_values, root_keys, root_values, parent, seg_blocks
):
    n_leaf = lax.axis_size("leaf")
    n_rep = lax.axis_size("rep")
    leaf_pos = lax.axis_index("leaf")
    rep_pos = lax.axis_index("rep")
    core = rep_pos % 2
    core_swap = [(r, r ^ 1) for r in range(n_rep)]

    def exchange(x):
        return lax.all_to_all(x, "leaf", 0, 0)

    def swap(x):
        return lax.ppermute(x, "rep", core_swap)

    row_parent = lax.dynamic_index_in_dim(parent.reshape(n_leaf, n_rep), rep_pos, 1, keepdims=False)
    row_blocks = lax.dynamic_index_in_dim(
        seg_blocks.reshape(n_leaf, n_rep), rep_pos, 1, keepdims=False
    )
    parent_two = jnp.where(row_parent >= 0, row_parent[jnp.maximum(row_parent, 0)], -1)
    sources = jnp.stack([parent_two, row_parent], axis=1)
    lens = jnp.where(sources >= 0, row_blocks[jnp.maximum(sources, 0)] * BLOCK, 0)
    info = jnp.concatenate(
        [lens[leaf_pos], (row_blocks[leaf_pos] * BLOCK)[None], core[None].astype(jnp.int32)]
    )
    sources = sources.reshape(-1)

    queries, attn_out, grad_out = queries[0], attn_out[0], grad_out[0]
    own_k, own_v = seg_keys[0], seg_values[0]

    core_info = jnp.concatenate([jnp.zeros((3,), jnp.int32), core[None].astype(jnp.int32)])
    send, rest = small_call(
        front_kernel, [(16, 256, 128), (128, 384)], "front",
        core_info, root_keys, root_values, own_k, own_v, from_hbm=True,
    )
    last_mine = lax.all_gather(rest[:, HEAD_DIM:], "leaf", axis=0, tiled=True)
    got = exchange(send)
    mine_0, send_first, send_rest = small_call(
        forward_kernel, [(16, 128, 128), (16, TERM_ROWS, 128), (16, 3 * TERM_ROWS + 128, 128)],
        "forward", jnp.concatenate([jnp.maximum(sources, 0), info]), got, rest,
    )
    other_0 = swap(mine_0)
    anc_0 = exchange(send_first)
    got_rest = exchange(send_rest)

    def run(head, column, anc_block, info, mine, other, anc):
        return head_call(
            head, column, anc_block, info, queries, grad_out, attn_out, mine, other, anc, own_k, own_v
        )

    info_0 = after(info, send_rest, anc_0)
    dq_0, keep_0, give_0, terms_0, own_0 = run(0, 0, 0, info_0, mine_0, other_0, anc_0)

    got_rest = after(got_rest, dq_0)
    mine_1 = got_rest[:, 3 * TERM_ROWS :]
    other_1 = swap(mine_1)
    info_1 = after(info, give_0)
    dq_1, keep_1, give_1, terms_1, own_1 = run(1, 0, 0, info_1, mine_1, other_1, got_rest)

    last_other = swap(after(last_mine, dq_0))
    got_0 = after(swap(give_0), dq_1)
    send_a = pack([(keep_0, got_0)], [terms_0, terms_1], "pack_a")
    info_2 = after(info, send_a)
    dq_2, keep_2, give_2, terms_2, own_2 = run(2, 0, 1, info_2, last_mine, last_other, got_rest)

    back_a = after(exchange(send_a), dq_2)
    got_1 = after(swap(give_1), dq_2)
    send_b = pack([(keep_1, got_1), (keep_2, swap(give_2))], [terms_2], "pack_b")
    info_3 = after(info, send_b)
    dq_3, keep_3, give_3, terms_3, own_3 = run(3, 1, 2, info_3, last_mine, last_other, got_rest)

    back_b = after(exchange(send_b), dq_3)
    send_c = pack([(keep_3, swap(give_3))], [terms_3], "pack_c")
    back_a, back_b = after(back_a, send_c), after(back_b, send_c)
    plane_a, sums_a = reduce_parts(1, 2, sources, back_a, (), "reduce_a")
    plane_b, sums_b = reduce_parts(2, 1, sources, back_b, (), "reduce_b")
    plane_c, sums = reduce_parts(1, 1, sources, exchange(send_c), (sums_a, sums_b), "reduce_c")
    back = exchange(sums)
    part = jnp.concatenate([plane_a, plane_b, plane_c], axis=0)
    shifted = []
    for shift in (1, 2, 3):
        perm = [(r, (r + 2 * shift) % n_rep) for r in range(n_rep)]
        shifted.append(lax.ppermute(part, "rep", perm))
    total = small_call(finish_root_kernel, [(128, 512)], "finish_root", part, *shifted)[0]
    swapped = swap(total)
    seg_k, seg_v = small_call(
        finish_seg_kernel, [(SEG_TOK, 512)] * 2, "finish_seg", back, own_0, own_1, own_2, own_3
    )
    return (
        jnp.concatenate([dq_0, dq_1, dq_2, dq_3], axis=1)[None],
        seg_k[None],
        seg_v[None],
        jnp.where(core == 0, total, swapped),
        jnp.where(core == 0, swapped, total),
    )


def solution(mesh):
    rows = P(("leaf", "rep"), None, None)
    root = P("leaf", None)
    return jax.shard_map(
        per_device,
        mesh=mesh,
        in_specs=(rows, rows, rows, rows, rows, root, root, P(), P()),
        out_specs=(rows, rows, rows, root, root),
        check_vma=False,
    )
```

```python
import functools
import math

import jax
import jax.numpy as jnp
from jax import lax
from jax.experimental import pallas as pl
from jax.experimental.pallas import tpu as pltpu
from jax.sharding import PartitionSpec as P

HEADS = 32
KV_HEADS = 4
HEAD_DIM = 128
BLOCK = 128
GROUP = HEADS // KV_HEADS
SEG_TOK = 256
ROOT = 2048
CHUNK = 256
KEYS = ROOT + 3 * SEG_TOK
PIECES = 16
PIECE = SEG_TOK // PIECES
TERM_ROWS = 4 * PIECE
SCALE = 1.0 / math.sqrt(HEAD_DIM)
SCALE_LOG2 = SCALE * math.log2(math.e)
BF16 = jnp.bfloat16
F32 = jnp.float32


def dot(a, b):
    return lax.dot_general(a, b, (((1,), (0,)), ((), ())), preferred_element_type=F32)


def head_kernel(
    per, info, q_ref, g_ref, o_ref, mine_ref, other_ref, anc_ref, own_k_ref, own_v_ref,
    dq_ref, keep_ref, give_ref, anc_out_ref, own_out_ref,
    k_rows, k_cols, v_cols, s_buf, e_buf, ds_buf, q_cols, g_cols, acc_k, acc_v,
):
    rows = per * SEG_TOK
    steps = GROUP // per
    n_root = ROOT // CHUNK
    n_chunk = KEYS // CHUNK
    two_len, one_len, own_len, core = info[0], info[1], info[2], info[3]
    first_core = core == 0

    def load_root(ref, j):
        if len(ref.shape) == 2:
            return ref[j * CHUNK : (j + 1) * CHUNK, :]
        per = CHUNK // ref.shape[1]
        return jnp.concatenate([ref[j * per + b] for b in range(per)], axis=0)

    for j in range(n_chunk):
        span = slice(j * CHUNK, (j + 1) * CHUNK)
        if j < n_root:
            mine, other = load_root(mine_ref, j), load_root(other_ref, j)
            k_tile = jnp.where(first_core, mine, other)
            v_tile = jnp.where(first_core, other, mine)
        elif j < n_root + 2:
            k_at, v_at = (j - n_root) * 2 * PIECE, ((j - n_root) * 2 + 1) * PIECE
            k_tile = jnp.concatenate([anc_ref[p, k_at : k_at + PIECE] for p in range(PIECES)], axis=0)
            v_tile = jnp.concatenate([anc_ref[p, v_at : v_at + PIECE] for p in range(PIECES)], axis=0)
        else:
            k_tile, v_tile = own_k_ref[...], own_v_ref[...]
        k_rows[span, :] = k_tile
        k_cols[:, span] = k_tile.T
        v_cols[:, span] = v_tile.T

    def stack(ref, i):
        return jnp.concatenate(
            [ref[:, (i * per + p) * HEAD_DIM : (i * per + p + 1) * HEAD_DIM] for p in range(per)],
            axis=0,
        )

    def row_ids():
        return lax.broadcasted_iota(jnp.int32, (rows, 1), 0) % SEG_TOK

    def scores(i):
        q = stack(q_ref, i)
        top = None
        for j in range(n_chunk):
            span = slice(j * CHUNK, (j + 1) * CHUNK)
            s = dot(q, k_cols[:, span])
            if j >= n_root:
                col = lax.broadcasted_iota(jnp.int32, (1, CHUNK), 1)
                if j == n_root:
                    live = col < two_len
                elif j == n_root + 1:
                    live = col < one_len
                else:
                    live = col <= row_ids()
                s = jnp.where(live, s, -jnp.inf)
            s_buf[i % 2, :, span] = s
            for w in range(0, CHUNK, 128):
                part = s[:, w : w + 128]
                top = part if top is None else jnp.maximum(top, part)
            yield None
        yield jnp.max(top, axis=-1, keepdims=True) * SCALE_LOG2

    def probs(i, top):
        g = jnp.where(row_ids() < own_len, stack(g_ref, i), jnp.zeros((), BF16))
        g_wide = g.astype(F32)
        delta = jnp.sum(g_wide * stack(o_ref, i).astype(F32), axis=-1, keepdims=True)
        dq = jnp.zeros((rows, HEAD_DIM), F32)
        total = None
        for j in range(n_chunk):
            span = slice(j * CHUNK, (j + 1) * CHUNK)
            e = jnp.exp2(s_buf[i % 2, :, span] * SCALE_LOG2 - top)
            for w in range(0, CHUNK, 128):
                part = e[:, w : w + 128]
                total = part if total is None else total + part
            e_buf[i % 2, :, span] = e.astype(BF16)
            dp = dot(g, v_cols[:, span])
            ds = (e * (dp - delta)).astype(BF16)
            ds_buf[i % 2, :, span] = ds
            dq = dq + dot(ds, k_rows[span, :])
            yield None
        inv = 1.0 / jnp.sum(total, axis=-1, keepdims=True)
        g_cols[i % 2] = (g_wide * inv).astype(BF16).T
        inv_scale = inv * SCALE
        q_cols[i % 2] = (stack(q_ref, i).astype(F32) * inv_scale).astype(BF16).T
        dq = dq * inv_scale
        for p in range(per):
            at = (i * per + p) * HEAD_DIM
            dq_ref[:, at : at + HEAD_DIM] = dq[p * SEG_TOK : (p + 1) * SEG_TOK].astype(BF16)
        yield None

    def keys(i):
        q, g = q_cols[i % 2], g_cols[i % 2]
        for j in range(n_chunk):
            span = slice(j * CHUNK, (j + 1) * CHUNK)
            dv = dot(g, e_buf[i % 2, :, span])
            dk = dot(q, ds_buf[i % 2, :, span])
            if i > 0:
                dv, dk = acc_v[:, span] + dv, acc_k[:, span] + dk
            if i < steps - 1:
                acc_v[:, span], acc_k[:, span] = dv, dk
            elif j < n_root:
                dk, dv = dk.astype(BF16), dv.astype(BF16)
                for w in range(0, CHUNK, 128):
                    block = (j * CHUNK + w) // 128
                    dk_tile, dv_tile = dk[:, w : w + 128], dv[:, w : w + 128]
                    keep_ref[block] = jnp.where(first_core, dk_tile, dv_tile)
                    give_ref[block] = jnp.where(first_core, dv_tile, dk_tile)
            else:
                dk, dv = dk.T.astype(BF16), dv.T.astype(BF16)
                if j < n_root + 2:
                    k_at, v_at = (j - n_root) * 2 * PIECE, ((j - n_root) * 2 + 1) * PIECE
                    for p in range(PIECES):
                        piece = slice(p * PIECE, (p + 1) * PIECE)
                        anc_out_ref[p, k_at : k_at + PIECE] = dk[piece]
                        anc_out_ref[p, v_at : v_at + PIECE] = dv[piece]
                else:
                    own_out_ref[:, :HEAD_DIM] = dk
                    own_out_ref[:, HEAD_DIM:] = dv
            yield None
        yield None

    tops = {}
    for step in range(-1, steps + 1):
        running = []
        if step + 1 < steps:
            running.append((step + 1, scores(step + 1)))
        if 0 <= step < steps:
            running.append((None, probs(step, tops[step])))
        if 0 <= step - 1:
            running.append((None, keys(step - 1)))
        for _ in range(n_chunk + 1):
            for tag, stream in running:
                value = next(stream)
                if value is not None:
                    tops[tag] = value


def head_call(head, root_column, anc_block, info, q, g, o, mine, other, anc, own_k, own_v):
    per = 1 if head > 0 else 2
    rows = per * SEG_TOK
    wide = GROUP * HEAD_DIM

    def full(shape):
        return pl.BlockSpec(shape, lambda i: (0,) * len(shape))

    def columns(height, width, at):
        return pl.BlockSpec((height, width), lambda i: (0, at))

    def root_spec(x):
        return full(x.shape) if x.ndim == 3 else columns(ROOT, HEAD_DIM, root_column)

    shapes = (
        (SEG_TOK, wide), (16, 128, 128), (16, 128, 128), (PIECES, TERM_ROWS, 128), (SEG_TOK, 256)
    )
    return pl.pallas_call(
        functools.partial(head_kernel, per),
        grid=(1,),
        in_specs=[
            pl.BlockSpec(memory_space=pltpu.SMEM),
            columns(SEG_TOK, wide, head),
            columns(SEG_TOK, wide, head),
            columns(SEG_TOK, wide, head),
            root_spec(mine),
            root_spec(other),
            pl.BlockSpec((PIECES, TERM_ROWS, 128), lambda i: (0, anc_block, 0)),
            columns(SEG_TOK, HEAD_DIM, head),
            columns(SEG_TOK, HEAD_DIM, head),
        ],
        out_specs=[full(s) for s in shapes],
        out_shape=[jax.ShapeDtypeStruct(s, BF16) for s in shapes],
        scratch_shapes=[
            pltpu.VMEM((KEYS, HEAD_DIM), BF16),
            pltpu.VMEM((HEAD_DIM, KEYS), BF16),
            pltpu.VMEM((HEAD_DIM, KEYS), BF16),
            pltpu.VMEM((2, rows, KEYS), F32),
            pltpu.VMEM((2, rows, KEYS), BF16),
            pltpu.VMEM((2, rows, KEYS), BF16),
            pltpu.VMEM((2, HEAD_DIM, rows), BF16),
            pltpu.VMEM((2, HEAD_DIM, rows), BF16),
            pltpu.VMEM((HEAD_DIM, KEYS), F32),
            pltpu.VMEM((HEAD_DIM, KEYS), F32),
        ],
        compiler_params=pltpu.CompilerParams(vmem_limit_bytes=60 * 2**20),
        cost_estimate=pl.CostEstimate(
            flops=5 * 2 * GROUP * SEG_TOK * KEYS * HEAD_DIM,
            bytes_accessed=50 * 2**20,
            transcendentals=GROUP * SEG_TOK * KEYS,
        ),
        name="head" + str(head),
    )(info, q, g, o, mine, other, anc, own_k, own_v)


def small_call(kernel, shapes, name, *args, scratch=(), from_hbm=False):
    smem = pl.BlockSpec(memory_space=pltpu.SMEM)
    vmem = pl.BlockSpec(memory_space=pltpu.VMEM)

    def spec(shape):
        return pl.BlockSpec(shape, lambda *i: (0,) * len(shape)) if from_hbm else vmem

    return pl.pallas_call(
        kernel,
        grid=(1,) if from_hbm else (),
        in_specs=[smem if a.dtype == jnp.int32 else spec(a.shape) for a in args],
        out_specs=[spec(s) for s in shapes],
        out_shape=[jax.ShapeDtypeStruct(s, BF16) for s in shapes],
        scratch_shapes=scratch,
        compiler_params=pltpu.CompilerParams(vmem_limit_bytes=(60 if from_hbm else 16) * 2**20),
        cost_estimate=pl.CostEstimate(flops=10**6, bytes_accessed=3 * 2**20, transcendentals=0),
        name=name,
    )(*args)


def front_kernel(info, root_k, root_v, own_k, own_v, send, rest):
    first_core = info[3] == 0
    mine = jnp.where(first_core, root_k[...], root_v[...])
    rest[...] = mine[:, HEAD_DIM:]
    for p in range(PIECES):
        send[p, :128] = mine[:, :HEAD_DIM]
        piece = slice(p * PIECE, (p + 1) * PIECE)
        for h in range(KV_HEADS):
            for c, part in enumerate((own_k, own_v)):
                at = 128 + (2 * h + c) * PIECE
                send[p, at : at + PIECE] = part[piece, h * HEAD_DIM : (h + 1) * HEAD_DIM]


def forward_kernel(wanted, got, rest, mine, send_first, send_rest):
    for p in range(PIECES):
        mine[p] = got[p, :128]
        send_rest[p, 3 * TERM_ROWS :] = rest[:, :HEAD_DIM]
        for w in range(2):
            source = wanted[2 * p + w]
            for h in range(KV_HEADS):
                rows = got[source, 128 + h * 2 * PIECE : 128 + (h + 1) * 2 * PIECE]
                if h == 0:
                    send_first[p, w * 2 * PIECE : (w + 1) * 2 * PIECE] = rows
                else:
                    at = (h - 1) * TERM_ROWS + w * 2 * PIECE
                    send_rest[p, at : at + 2 * PIECE] = rows


def pack_kernel(n_root, n_terms, *refs):
    out = refs[-1]
    for i in range(n_root):
        keep, got = refs[2 * i], refs[2 * i + 1]
        for b in range(16):
            total = keep[b].astype(F32) + got[b].astype(F32)
            out[b, i * 128 : (i + 1) * 128] = total.astype(BF16)
    for i in range(n_terms):
        at = n_root * 128 + i * TERM_ROWS
        out[:, at : at + TERM_ROWS] = refs[2 * n_root + i][...]


def pack(roots, terms, name):
    n_root, n_terms = len(roots), len(terms)
    rows = n_root * 128 + n_terms * TERM_ROWS
    flat = [x for pair in roots for x in pair] + list(terms)
    return small_call(
        functools.partial(pack_kernel, n_root, n_terms), [(16, rows, 128)], name, *flat
    )[0]


def reduce_kernel(n_root, n_terms, n_before, sources, got, *refs):
    before, planes, sums, acc = refs[:n_before], refs[n_before], refs[n_before + 1], refs[-1]
    for i in range(n_root):
        total = got[0, i * 128 : (i + 1) * 128].astype(F32)
        for d in range(1, 16):
            total += got[d, i * 128 : (i + 1) * 128].astype(F32)
        planes[i] = total.astype(BF16)
    acc[...] = jnp.zeros_like(acc)
    for d in range(16):
        for w in range(2):
            target = sources[2 * d + w]

            @pl.when(target >= 0)
            def _():
                for i in range(n_terms):
                    at = n_root * 128 + i * TERM_ROWS + w * 2 * PIECE
                    rows = slice(i * 2 * PIECE, (i + 1) * 2 * PIECE)
                    acc[target, rows] += got[d, at : at + 2 * PIECE].astype(F32)

    at = 0
    for ref in before:
        height = ref.shape[1]
        sums[:, at : at + height] = ref[...]
        at += height
    sums[:, at:] = acc[...].astype(BF16)


def reduce_parts(n_root, n_terms, sources, got, before, name):
    rows = n_terms * 2 * PIECE + sum(b.shape[1] for b in before)
    return small_call(
        functools.partial(reduce_kernel, n_root, n_terms, len(before)),
        [(n_root, 128, 128), (16, rows, 128)],
        name, sources, got, *before,
        scratch=[pltpu.VMEM((16, n_terms * 2 * PIECE, 128), F32)],
    )


def finish_seg_kernel(back, *refs):
    own, out_k, out_v = refs[:-2], refs[-2], refs[-1]
    for h in range(KV_HEADS):
        cols = slice(h * HEAD_DIM, (h + 1) * HEAD_DIM)
        for p in range(PIECES):
            piece = slice(p * PIECE, (p + 1) * PIECE)
            for c, out in enumerate((out_k, out_v)):
                at = (2 * h + c) * PIECE
                term = own[h][piece, c * HEAD_DIM : (c + 1) * HEAD_DIM]
                total = back[p, at : at + PIECE].astype(F32) + term.astype(F32)
                out[piece, cols] = total.astype(BF16)


def finish_root_kernel(*refs):
    out = refs[-1]
    for h in range(KV_HEADS):
        total = refs[0][h].astype(F32)
        for ref in refs[1:-1]:
            total += ref[h].astype(F32)
        out[:, h * HEAD_DIM : (h + 1) * HEAD_DIM] = total.T.astype(BF16)


def after(x, *deps):
    return lax.optimization_barrier((x,) + deps)[0]


def per_device(
    queries, attn_out, grad_out, seg_keys, seg_values, root_keys, root_values, parent, seg_blocks
):
    n_leaf = lax.axis_size("leaf")
    n_rep = lax.axis_size("rep")
    leaf_pos = lax.axis_index("leaf")
    rep_pos = lax.axis_index("rep")
    core = rep_pos % 2
    core_swap = [(r, r ^ 1) for r in range(n_rep)]

    def exchange(x):
        return lax.all_to_all(x, "leaf", 0, 0)

    def swap(x):
        return lax.ppermute(x, "rep", core_swap)

    row_parent = lax.dynamic_index_in_dim(parent.reshape(n_leaf, n_rep), rep_pos, 1, keepdims=False)
    row_blocks = lax.dynamic_index_in_dim(
        seg_blocks.reshape(n_leaf, n_rep), rep_pos, 1, keepdims=False
    )
    parent_two = jnp.where(row_parent >= 0, row_parent[jnp.maximum(row_parent, 0)], -1)
    sources = jnp.stack([parent_two, row_parent], axis=1)
    lens = jnp.where(sources >= 0, row_blocks[jnp.maximum(sources, 0)] * BLOCK, 0)
    info = jnp.concatenate(
        [lens[leaf_pos], (row_blocks[leaf_pos] * BLOCK)[None], core[None].astype(jnp.int32)]
    )
    sources = sources.reshape(-1)

    queries, attn_out, grad_out = queries[0], attn_out[0], grad_out[0]
    own_k, own_v = seg_keys[0], seg_values[0]

    core_info = jnp.concatenate([jnp.zeros((3,), jnp.int32), core[None].astype(jnp.int32)])
    send, rest = small_call(
        front_kernel, [(16, 256, 128), (128, 384)], "front",
        core_info, root_keys, root_values, own_k, own_v, from_hbm=True,
    )
    last_mine = lax.all_gather(rest[:, HEAD_DIM:], "leaf", axis=0, tiled=True)
    got = exchange(send)
    mine_0, send_first, send_rest = small_call(
        forward_kernel, [(16, 128, 128), (16, TERM_ROWS, 128), (16, 3 * TERM_ROWS + 128, 128)],
        "forward", jnp.concatenate([jnp.maximum(sources, 0), info]), got, rest,
    )
    other_0 = swap(mine_0)
    anc_0 = exchange(send_first)
    got_rest = exchange(send_rest)

    def run(head, column, anc_block, info, mine, other, anc):
        return head_call(
            head, column, anc_block, info, queries, grad_out, attn_out, mine, other, anc, own_k, own_v
        )

    info_0 = after(info, send_rest, anc_0)
    dq_0, keep_0, give_0, terms_0, own_0 = run(0, 0, 0, info_0, mine_0, other_0, anc_0)

    got_rest = after(got_rest, dq_0)
    mine_1 = got_rest[:, 3 * TERM_ROWS :]
    other_1 = swap(mine_1)
    info_1 = after(info, give_0)
    dq_1, keep_1, give_1, terms_1, own_1 = run(1, 0, 0, info_1, mine_1, other_1, got_rest)

    last_other = swap(after(last_mine, dq_0))
    got_0 = after(swap(give_0), dq_1)
    info_2 = after(info, dq_1)
    dq_2, keep_2, give_2, terms_2, own_2 = run(2, 0, 1, info_2, last_mine, last_other, got_rest)

    got_1 = after(swap(give_1), dq_2)
    send_b = pack([(keep_0, got_0), (keep_1, got_1)], [terms_0, terms_1, terms_2], "pack_b")
    info_3 = after(info, send_b)
    dq_3, keep_3, give_3, terms_3, own_3 = run(3, 1, 2, info_3, last_mine, last_other, got_rest)

    back_b = after(exchange(send_b), dq_3)
    got_2 = after(swap(give_2), dq_3)
    send_c = pack([(keep_2, got_2), (keep_3, swap(give_3))], [terms_3], "pack_c")
    back_b = after(back_b, send_c)
    plane_b, sums_b = reduce_parts(2, 3, sources, back_b, (), "reduce_b")
    plane_c, sums = reduce_parts(2, 1, sources, exchange(send_c), (sums_b,), "reduce_c")
    back = exchange(sums)
    part = jnp.concatenate([plane_b, plane_c], axis=0)
    shifted = []
    for shift in (1, 2, 3):
        perm = [(r, (r + 2 * shift) % n_rep) for r in range(n_rep)]
        shifted.append(lax.ppermute(part, "rep", perm))
    total = small_call(finish_root_kernel, [(128, 512)], "finish_root", part, *shifted)[0]
    swapped = swap(total)
    seg_k, seg_v = small_call(
        finish_seg_kernel, [(SEG_TOK, 512)] * 2, "finish_seg", back, own_0, own_1, own_2, own_3
    )
    return (
        jnp.concatenate([dq_0, dq_1, dq_2, dq_3], axis=1)[None],
        seg_k[None],
        seg_v[None],
        jnp.where(core == 0, total, swapped),
        jnp.where(core == 0, swapped, total),
    )


def solution(mesh):
    rows = P(("leaf", "rep"), None, None)
    root = P("leaf", None)
    return jax.shard_map(
        per_device,
        mesh=mesh,
        in_specs=(rows, rows, rows, rows, rows, root, root, P(), P()),
        out_specs=(rows, rows, rows, root, root),
        check_vma=False,
    )
```
